32 devices in a mesh: group: 2 (over x), tile: 16 (over z, y, core).
Axes of the slice: x: 2, y: 2, z: 4, core: 2. Of those that a mesh axis runs over, the one named last changes fastest.
Arguments:
- gains: float32 [32768, 64], P(('group', 'tile')), parts along dimension 0, may hold values from -6 to 6
- tiles: int32 [256, 3], P(('group', 'tile')), parts along dimension 0, may hold values from 0 to 15, as said below
- vis: bfloat16 [256, 2, 32, 1024], P(('group', 'tile')), parts along dimension 0, may hold values from -24 to 24
- flags: int32 [256, 1024], P(('group', 'tile')), parts along dimension 0, may hold values 0 or 1
- station_uvw: float32 [32, 3, 512], P('group'), parts along dimension 0, may hold values from -1000 to 1000
- src_lm: float32 [2, 32], replicated, may hold values from -0.02 to 0.02
- flux: float32 [32, 32], replicated, may hold values from 0.2 to 2
Outputs:
- gains_out: float32 [32768, 64], P(('group', 'tile')), parts along dimension 0
The draws below stay inside these ranges and needn't reach their ends.
There are 2 independent parts, one for each index of `group`. The reference program is written for one: setup_inputs(seed, part) draws one part's arguments, and reference() takes and returns one part's arrays. A program takes and returns all parts, laid end to end along the dimension named above; an argument that names none is the same for every part. Nothing has to cross between parts.
Inputs may be any that keep to these rules, and one draw needn't show every extreme that they name: `tiles`: each row is (row block, column block, time step) of one item; the row block is at least the column block, both below 16, and the time step is below 16.
All inputs are finite; a program needn't handle non-finite values. No bound on the sum of `flags` on one device may be relied on, other than what follows from the above.
Results may differ from the reference program's by a relative error of at most 0.0013.
Values sent between devices are 32-bit elements; how exact they have to be, the bound alone decides.
A program may use at most 192 MiB of HBM per device.

```python
import math
import jax
import jax.numpy as jnp
from jax import lax

STATIONS = 512
DIRS = 32
CHANS = 32
SB = 32
TIMES = 16
ITERS = 2
SLOT_DEV = 8
SLOTS = 128
N_TILE = 16


def draw_tiles(key, part):
    key = jax.random.fold_in(key, 11)
    key_first, key_second, key_steps = jax.random.split(key, 3)
    block_count = STATIONS // SB
    first = jax.random.randint(key_first, (SLOTS,), 0, block_count)
    second = jax.random.randint(key_second, (SLOTS,), 0, block_count)
    upper = jnp.maximum(first, second).at[0].set(block_count - 1)
    lower = jnp.minimum(first, second).at[0].set(0)
    step_ids = jax.random.randint(key_steps, (SLOTS,), 0, TIMES).at[0].set(TIMES - 1)
    return jnp.stack([upper, lower, step_ids], axis=1).astype(jnp.int32)


def with_ends(drawn, key, smallest, top_value):
    place = [jax.random.randint(jax.random.fold_in(key, axis), (), 0, length) for axis, length in enumerate(drawn.shape)]
    main_axis = drawn.shape.index(max(drawn.shape))
    next_to = place[:main_axis] + [(place[main_axis] + 1) % drawn.shape[main_axis]] + place[main_axis + 1:]
    return drawn.at[tuple(place)].set(smallest).at[tuple(next_to)].set(top_value)


def level_of(rng, dims, cuts, smallest, high):
    def one(dim, blocks):
        draws = jax.random.uniform(jax.random.fold_in(jax.random.fold_in(rng, 6), dim), (blocks,), jnp.float32, smallest / len(cuts), high / len(cuts))
        return jnp.repeat(jnp.exp(draws), dims[dim] // blocks).reshape((-1,) + (1,) * (len(dims) - dim - 1))

    loudness = one(*cuts[0])
    for cut in cuts[1:]:
        loudness = loudness * one(*cut)
    return loudness


def gaussian(own_key, shape, width, bound, shards=(), kind=jnp.bfloat16):
    factor_of = level_of(own_key, shape, shards, -0.22, 0.18) if shards else 1.0
    array = jax.random.normal(own_key, shape, jnp.float32) * width * factor_of
    return jnp.minimum(jnp.maximum(array, -bound), bound).astype(kind)


def setup_inputs(seed: int = 0, part: int = 0) -> dict:
    keys = jax.random.split(jax.random.key(seed), 8)
    own_keys = jax.random.split(jax.random.fold_in(keys[7], part), 8)
    gains = gaussian(own_keys[0], (STATIONS * DIRS, 2 * CHANS), 1.0, 6.0, ((0, 16),), jnp.float32)
    tiles = draw_tiles(jax.random.fold_in(jax.random.fold_in(keys[7], part), 71), part)
    vis = gaussian(own_keys[2], (SLOTS, 2, CHANS, SB * SB), 4.0, 24.0, ((0, 16),))
    flags = with_ends((jax.random.randint(own_keys[3], (SLOTS, SB * SB), 0, 8) < 7).astype(jnp.int32), jax.random.fold_in(own_keys[3], 1), 0, 1)
    station_uvw = jnp.clip(jax.random.uniform(own_keys[4], (TIMES, 3, STATIONS), jnp.float32, -1000.0, 1000.0), -1000.0, 1000.0)
    src_lm = jnp.clip(jax.random.uniform(keys[5], (2, DIRS), jnp.float32, -0.02, 0.02), -0.02, 0.02)
    flux = jnp.clip(jnp.exp(jax.random.uniform(keys[6], (DIRS, CHANS), jnp.float32, math.log(0.2), math.log(2.0))), 0.2, 2.0)
    return dict(gains=gains, tiles=tiles, vis=vis, flags=flags, station_uvw=station_uvw, src_lm=src_lm, flux=flux)


highest = lax.Precision.HIGHEST

def product(form, left, right):
    return jnp.einsum(form, left, right, precision=highest)

def rotate(positions, gain_block, source_l, source_m, source_n, frequency):
    delays = positions[:, 0, :, None] * source_l + positions[:, 1, :, None] * source_m + positions[:, 2, :, None] * source_n
    phases = 2.0 * math.pi * delays[:, None, :, :] * frequency[None, :, None, None]
    cosine = jnp.cos(phases)
    sine_part = jnp.sin(phases)
    gain_re = jnp.transpose(gain_block[:, :, :, 0, :], (0, 3, 1, 2))
    gain_im = jnp.transpose(gain_block[:, :, :, 1, :], (0, 3, 1, 2))
    rotated_re = gain_re * cosine - gain_im * sine_part
    rotated_im = gain_re * sine_part + gain_im * cosine
    return (cosine, sine_part, rotated_re, rotated_im)

def normal_terms(gains_full, tiles, vis, flags, station_uvw, src_lm, flux):
    item_count = tiles.shape[0]
    block_count = STATIONS // SB
    blocks = gains_full.reshape(block_count, SB, DIRS, 2, CHANS)
    row_block = tiles[:, 0]
    col_block = tiles[:, 1]
    step_index = tiles[:, 2]
    labels = jnp.arange(block_count, dtype=jnp.int32)
    pick_row = (row_block[:, None] == labels[None, :]).astype(jnp.float32)
    pick_col = (col_block[:, None] == labels[None, :]).astype(jnp.float32)
    positions = station_uvw[step_index].reshape(item_count, 3, block_count, SB)
    row_uvw = product('nb,nxbs->nxs', pick_row, positions)
    col_uvw = product('nb,nxbs->nxs', pick_col, positions)
    source_l = src_lm[0]
    source_m = src_lm[1]
    source_n = jnp.sqrt(1.0 - source_l * source_l - source_m * source_m) - 1.0
    frequency = 1.0 + jnp.arange(CHANS, dtype=jnp.float32) / CHANS
    row_cos, row_sin, row_re, row_im = rotate(row_uvw, blocks[row_block], source_l, source_m, source_n, frequency)
    col_cos, col_sin, col_re, col_im = rotate(col_uvw, blocks[col_block], source_l, source_m, source_n, frequency)
    flux_weight = jnp.transpose(flux)[None, :, None, :]
    scaled_re = row_re * flux_weight
    scaled_im = row_im * flux_weight
    model_re = product('nfrk,nfck->nfrc', scaled_re, col_re) + product('nfrk,nfck->nfrc', scaled_im, col_im)
    model_im = product('nfrk,nfck->nfrc', scaled_im, col_re) - product('nfrk,nfck->nfrc', scaled_re, col_im)
    row_local = jnp.arange(SB, dtype=jnp.int32)
    lower_part = (row_local[:, None] > row_local[None, :])[None, :, :]
    distinct = (row_block != col_block)[:, None, None]
    keep = jnp.logical_or(distinct, lower_part).astype(jnp.float32)
    baseline_mask = flags.reshape(item_count, SB, SB).astype(jnp.float32) * keep
    observed = vis.astype(jnp.float32).reshape(item_count, 2, CHANS, SB, SB)
    resid_re = (observed[:, 0] - model_re) * baseline_mask[:, None]
    resid_im = (observed[:, 1] - model_im) * baseline_mask[:, None]
    srow_re = product('nfrc,nfck->nfrk', resid_re, col_re) - product('nfrc,nfck->nfrk', resid_im, col_im)
    srow_im = product('nfrc,nfck->nfrk', resid_re, col_im) + product('nfrc,nfck->nfrk', resid_im, col_re)
    scol_re = product('nfrc,nfrk->nfck', resid_re, row_re) + product('nfrc,nfrk->nfck', resid_im, row_im)
    scol_im = product('nfrc,nfrk->nfck', resid_re, row_im) - product('nfrc,nfrk->nfck', resid_im, row_re)
    nrow_re = flux_weight * (row_cos * srow_re + row_sin * srow_im)
    nrow_im = flux_weight * (row_cos * srow_im - row_sin * srow_re)
    ncol_re = flux_weight * (col_cos * scol_re + col_sin * scol_im)
    ncol_im = flux_weight * (col_cos * scol_im - col_sin * scol_re)
    flux_power = flux_weight * flux_weight
    drow = flux_power * product('nrc,nfck->nfrk', baseline_mask, col_re * col_re + col_im * col_im)
    dcol = flux_power * product('nrc,nfrk->nfck', baseline_mask, row_re * row_re + row_im * row_im)

    def deposit(row_term, col_term):
        summed = product('nb,nfrk->brkf', pick_row, row_term) + product('nb,nfrk->brkf', pick_col, col_term)
        return summed.reshape(STATIONS * DIRS, CHANS)
    numerator = jnp.concatenate([deposit(nrow_re, ncol_re), deposit(nrow_im, ncol_im)], axis=1)
    denominator = deposit(drow, dcol)
    return (numerator, denominator)

def refine(current, numerator, denominator):
    return current + 0.5 * numerator / (jnp.concatenate([denominator, denominator], axis=1) + 1.0)

def reference(gains, tiles, vis, flags, station_uvw, src_lm, flux):
    current = gains
    groups = (tiles.reshape(N_TILE, SLOT_DEV, 3), vis.reshape(N_TILE, SLOT_DEV, 2, CHANS, SB * SB), flags.reshape(N_TILE, SLOT_DEV, SB * SB))
    for iteration in range(ITERS):

        def accumulate(carry, group, current=current):
            numerator, denominator = normal_terms(current, group[0], group[1], group[2], station_uvw, src_lm, flux)
            return ((carry[0] + numerator, carry[1] + denominator), None)
        start_sums = (jnp.zeros((STATIONS * DIRS, 2 * CHANS), jnp.float32), jnp.zeros((STATIONS * DIRS, CHANS), jnp.float32))
        (numerator, denominator), unused = lax.scan(accumulate, start_sums, groups)
        current = refine(current, numerator, denominator)
    return current
```

```python
import functools
import math

import jax
import jax.numpy as jnp
from jax import lax
from jax.experimental import pallas as pl
from jax.experimental.pallas import tpu as pltpu
from jax.sharding import PartitionSpec as P

SB = 32
ITERS = 2
GROUPS = 2
LANES = 128
VMEM = 40 * 1024 * 1024

highest = lax.Precision.HIGHEST


def series(first, step, terms):
    out = []
    for j in range(terms):
        degree = first + step * j
        out.append((-1.0) ** j * math.pi**degree / math.factorial(degree))
    return out


SIN = series(1, 2, 7)
COS = series(0, 2, 7)


def horner(coefficients, z):
    total = jnp.full_like(z, coefficients[-1])
    for value in reversed(coefficients[:-1]):
        total = total * z + value
    return total


def phasor_kernel(tiles_ref, uvw_ref, lanes_ref, cos_ref, sin_ref):
    uvw = uvw_ref[0, 0]
    u, v, w = uvw[:, 0:1], uvw[:, 1:2], uvw[:, 2:3]
    width = lanes_ref.shape[1]
    for start in range(0, width, 256):
        cut = slice(start, start + 256)
        delay = u * lanes_ref[0:1, cut] + v * lanes_ref[1:2, cut] + w * lanes_ref[2:3, cut]
        turns = delay * lanes_ref[3:4, cut]
        r = turns - jnp.floor(turns + 0.5)
        z = r * r
        s = r * horner(SIN, z)
        c = horner(COS, z)
        cos_ref[0, :, cut] = 1.0 - 2.0 * s * s
        sin_ref[0, :, cut] = 2.0 * s * c


def phasors(tiles, uvw_columns, lane_rows):
    items = tiles.shape[0]
    width = lane_rows.shape[1]

    def pick(i, t):
        return (t[i // 2, 2], t[i // 2, i % 2], 0, 0)

    shape = jax.ShapeDtypeStruct((2 * items, SB, width), jnp.float32)
    block = pl.BlockSpec((1, SB, width), lambda i, t: (i, 0, 0))
    return pl.pallas_call(
        phasor_kernel,
        grid_spec=pltpu.PrefetchScalarGridSpec(
            num_scalar_prefetch=1,
            grid=(2 * items,),
            in_specs=[
                pl.BlockSpec((1, 1, SB, 3), pick),
                pl.BlockSpec((8, width), lambda i, t: (0, 0)),
            ],
            out_specs=[block, block],
        ),
        out_shape=[shape, shape],
        compiler_params=pltpu.CompilerParams(vmem_limit_bytes=VMEM),
        cost_estimate=pl.CostEstimate(
            flops=2 * items * SB * width * 40,
            bytes_accessed=2 * items * SB * width * 8,
            transcendentals=0,
        ),
    )(tiles, uvw_columns, lane_rows)


def split(x):
    high = x.astype(jnp.bfloat16)
    return high, (x - high.astype(jnp.float32)).astype(jnp.bfloat16)


def dot(left, right, left_dim, right_dim):
    def one(a, b):
        return lax.dot_general(
            a,
            b,
            (((left_dim,), (right_dim,)), ((), ())),
            preferred_element_type=jnp.float32,
        )

    return one(left[0], right[0]) + (one(left[0], right[1]) + one(left[1], right[0]))


def normal_kernel(
    tiles_ref, grow_ref, gcol_ref, cos_ref, sin_ref, vis_ref, w_ref, flux_ref, out_ref
):
    item = pl.program_id(0)

    @pl.when(item == 0)
    def _():
        out_ref[...] = jnp.zeros_like(out_ref)

    width = flux_ref.shape[1]
    row_block = tiles_ref[item, 0]
    col_block = tiles_ref[item, 1]
    weights = jnp.concatenate([w_ref[0]] * 4, axis=0)
    own = (
        lax.broadcasted_iota(jnp.int32, (LANES, LANES), 0) // SB
        == lax.broadcasted_iota(jnp.int32, (LANES, LANES), 1) // SB
    )
    mask = own.astype(jnp.float32)
    mask_half = mask.astype(jnp.bfloat16)
    for start in range(0, width, LANES):
        re = slice(start, start + LANES)
        im = slice(width + start, width + start + LANES)
        flux = flux_ref[:, re]
        cr, sr = cos_ref[0, :, re], sin_ref[0, :, re]
        cc, sc = cos_ref[1, :, re], sin_ref[1, :, re]
        a_re, a_im = grow_ref[0, :, re], grow_ref[0, :, im]
        b_re, b_im = gcol_ref[0, :, re], gcol_ref[0, :, im]
        row_re, row_im = split(a_re * cr - a_im * sr), split(a_re * sr + a_im * cr)
        col_re = split(flux * (b_re * cc - b_im * sc))
        col_im = split(flux * (b_re * sc + b_im * cc))
        rows = [
            jnp.concatenate(
                [
                    jnp.concatenate([row_re[j]] * 4, axis=0) * mask_half,
                    jnp.concatenate([row_im[j]] * 4, axis=0) * mask_half,
                ],
                axis=1,
            )
            for j in range(2)
        ]
        cols = [
            jnp.concatenate(
                [
                    jnp.concatenate([col_re[j], col_im[j]], axis=1),
                    jnp.concatenate([-col_im[j], col_re[j]], axis=1),
                ],
                axis=0,
            )
            for j in range(2)
        ]
        model = dot(rows, cols, 1, 1)
        observed = vis_ref[0, start : start + LANES, :].astype(jnp.float32)
        resid = split((observed - model) * weights)
        srow = dot(resid, cols, 1, 0)
        cross = dot(resid, rows, 0, 0)
        s_re, s_im = srow[:, :LANES] * mask, srow[:, LANES:] * mask
        s_re = (s_re[0:32] + s_re[32:64]) + (s_re[64:96] + s_re[96:128])
        s_im = (s_im[0:32] + s_im[32:64]) + (s_im[64:96] + s_im[96:128])
        t_re = flux * (cross[:SB, :LANES] + cross[SB:, LANES:])
        t_im = flux * (cross[:SB, LANES:] - cross[SB:, :LANES])
        out_ref[row_block, :, re] += cr * s_re + sr * s_im
        out_ref[row_block, :, im] += cr * s_im - sr * s_re
        out_ref[col_block, :, re] += cc * t_re + sc * t_im
        out_ref[col_block, :, im] += cc * t_im - sc * t_re


def normal_terms(group, tiles, gathered, cosine, sine_part, vis_rows, weights, flux_row):
    items = tiles.shape[0]
    width = flux_row.shape[1]
    blocks = gathered.shape[0]
    gain_spec = lambda side: pl.BlockSpec(
        (1, SB, 2 * width), lambda i, t: (t[i, side], 0, 0)
    )
    turn_spec = pl.BlockSpec((2, SB, width), lambda i, t: (i, 0, group))
    return pl.pallas_call(
        normal_kernel,
        grid_spec=pltpu.PrefetchScalarGridSpec(
            num_scalar_prefetch=1,
            grid=(items,),
            in_specs=[
                gain_spec(0),
                gain_spec(1),
                turn_spec,
                turn_spec,
                pl.BlockSpec((1, width, 2 * SB), lambda i, t: (i, group, 0)),
                pl.BlockSpec((1, SB, 2 * SB), lambda i, t: (i, 0, 0)),
                pl.BlockSpec((1, width), lambda i, t: (0, 0)),
            ],
            out_specs=pl.BlockSpec((blocks, SB, 2 * width), lambda i, t: (0, 0, 0)),
        ),
        out_shape=jax.ShapeDtypeStruct((blocks, SB, 2 * width), jnp.float32),
        compiler_params=pltpu.CompilerParams(vmem_limit_bytes=VMEM),
        cost_estimate=pl.CostEstimate(
            flops=items * width * 3 * 8 * SB * SB * 24,
            bytes_accessed=items * width * SB * 30 + blocks * SB * width * 8,
            transcendentals=0,
        ),
    )(tiles, gathered, gathered, cosine, sine_part, vis_rows, weights, flux_row)


def on_device(gains, tiles, vis, flags, station_uvw, src_lm, flux):
    dirs, chans = flux.shape
    times, _, stations = station_uvw.shape
    items = tiles.shape[0]
    blocks = stations // SB
    owned_count = gains.shape[0] // dirs
    per = chans // GROUPS
    width = per * dirs

    turned = gains.reshape(owned_count, dirs, 2, GROUPS, per).transpose(3, 0, 2, 4, 1)
    owned = [turned[g].reshape(owned_count, 2 * width) for g in range(GROUPS)]

    def gather(x):
        return lax.all_gather(x, "tile", axis=0, tiled=True)

    gathered = [gather(x) for x in owned]

    keep = jnp.logical_or(
        (tiles[:, 0] != tiles[:, 1])[:, None],
        (jnp.arange(SB)[:, None] > jnp.arange(SB)[None, :]).reshape(1, SB * SB),
    )
    weights = jnp.where(keep, flags, 0).astype(jnp.float32)
    all_weights = gather(weights)
    all_tiles = gather(tiles)

    source_l, source_m = src_lm[0], src_lm[1]
    squares = source_l * source_l + source_m * source_m
    source_n = -squares / (1.0 + jnp.sqrt(1.0 - squares))
    frequency = 1.0 + jnp.arange(chans, dtype=jnp.float32) / chans
    lane_rows = jnp.stack(
        [jnp.tile(source_l, chans), jnp.tile(source_m, chans), jnp.tile(source_n, chans)]
        + [jnp.repeat(frequency, dirs)] * 5
    )
    uvw_columns = station_uvw.reshape(times, 3, blocks, SB).transpose(0, 2, 3, 1)
    cosine, sine_part = phasors(tiles, uvw_columns, lane_rows)

    vis_rows = vis.reshape(items, 2, chans, SB, SB).transpose(0, 2, 3, 1, 4)
    vis_rows = vis_rows.reshape(items, chans * SB, 2 * SB)
    square = weights.reshape(items, SB, SB)
    pair_weights = jnp.concatenate([square, square], axis=2)
    flux_rows = flux.T.reshape(GROUPS, 1, width)

    first = lax.axis_index("tile") * owned_count
    block, offset = first // SB, first % SB
    labels = jnp.arange(blocks, dtype=jnp.int32)[None, :]
    is_row = (all_tiles[:, 0:1] == block) & (all_tiles[:, 1:2] == labels)
    is_col = (all_tiles[:, 1:2] == block) & (all_tiles[:, 0:1] == labels)
    as_row = jnp.einsum(
        "ib,ix->bx", is_row.astype(jnp.float32), all_weights, precision=highest
    ).reshape(blocks, SB, SB)
    as_col = jnp.einsum(
        "ib,ix->bx", is_col.astype(jnp.float32), all_weights, precision=highest
    ).reshape(blocks, SB, SB)
    as_row = lax.dynamic_slice_in_dim(as_row, offset, owned_count, 1)
    as_col = lax.dynamic_slice_in_dim(as_col, offset, owned_count, 2)
    pair_counts = (as_row.transpose(1, 0, 2) + as_col.transpose(2, 0, 1)).reshape(
        owned_count, stations
    )

    for iteration in range(ITERS):
        updated = []
        for g in range(GROUPS):
            full = gathered[g]
            numerator = normal_terms(
                g,
                tiles,
                full.reshape(blocks, SB, 2 * width),
                cosine,
                sine_part,
                vis_rows,
                pair_weights,
                flux_rows[g],
            ).reshape(stations, 2 * width)
            share = lax.psum_scatter(numerator, "tile", scatter_dimension=0, tiled=True)
            power = full[:, :width] * full[:, :width] + full[:, width:] * full[:, width:]
            denominator = (flux_rows[g] * flux_rows[g]) * jnp.dot(
                pair_counts, power, precision=highest
            )
            scale = 0.5 / (denominator + 1.0)
            updated.append(owned[g] + share * jnp.concatenate([scale, scale], axis=1))
        owned = updated
        if iteration + 1 < ITERS:
            gathered = [gather(x) for x in owned]

    stacked = jnp.stack(owned).reshape(GROUPS, owned_count, 2, per, dirs)
    return stacked.transpose(1, 4, 2, 0, 3).reshape(owned_count * dirs, 2 * chans)


def solution(mesh):
    placed = (
        P(("group", "tile"), None),
        P(("group", "tile"), None),
        P(("group", "tile"), None, None, None),
        P(("group", "tile"), None),
        P("group", None, None),
        P(),
        P(),
    )
    return jax.shard_map(
        on_device, mesh=mesh, in_specs=placed, out_specs=P(("group", "tile"), None), check_vma=False
    )
```

```python
import functools
import math

import jax
import jax.numpy as jnp
from jax import lax
from jax.experimental import pallas as pl
from jax.experimental.pallas import tpu as pltpu
from jax.sharding import PartitionSpec as P

SB = 32
ITERS = 2
GROUPS = 1
LANES = 128
VMEM = 40 * 1024 * 1024

highest = lax.Precision.HIGHEST


def series(first, step, terms):
    out = []
    for j in range(terms):
        degree = first + step * j
        out.append((-1.0) ** j * math.pi**degree / math.factorial(degree))
    return out


SIN = series(1, 2, 7)
COS = series(0, 2, 7)


def horner(coefficients, z):
    total = jnp.full_like(z, coefficients[-1])
    for value in reversed(coefficients[:-1]):
        total = total * z + value
    return total


def phasor_kernel(tiles_ref, uvw_ref, lanes_ref, cos_ref, sin_ref):
    uvw = uvw_ref[0, 0]
    u, v, w = uvw[:, 0:1], uvw[:, 1:2], uvw[:, 2:3]
    width = lanes_ref.shape[1]
    for start in range(0, width, 256):
        cut = slice(start, start + 256)
        delay = u * lanes_ref[0:1, cut] + v * lanes_ref[1:2, cut] + w * lanes_ref[2:3, cut]
        turns = delay * lanes_ref[3:4, cut]
        r = turns - jnp.floor(turns + 0.5)
        z = r * r
        s = r * horner(SIN, z)
        c = horner(COS, z)
        cos_ref[0, :, cut] = 1.0 - 2.0 * s * s
        sin_ref[0, :, cut] = 2.0 * s * c


def phasors(tiles, uvw_columns, lane_rows):
    items = tiles.shape[0]
    width = lane_rows.shape[1]

    def pick(i, t):
        return (t[i // 2, 2], t[i // 2, i % 2], 0, 0)

    shape = jax.ShapeDtypeStruct((2 * items, SB, width), jnp.float32)
    block = pl.BlockSpec((1, SB, width), lambda i, t: (i, 0, 0))
    return pl.pallas_call(
        phasor_kernel,
        grid_spec=pltpu.PrefetchScalarGridSpec(
            num_scalar_prefetch=1,
            grid=(2 * items,),
            in_specs=[
                pl.BlockSpec((1, 1, SB, 3), pick),
                pl.BlockSpec((8, width), lambda i, t: (0, 0)),
            ],
            out_specs=[block, block],
        ),
        out_shape=[shape, shape],
        compiler_params=pltpu.CompilerParams(vmem_limit_bytes=VMEM),
        cost_estimate=pl.CostEstimate(
            flops=2 * items * SB * width * 40,
            bytes_accessed=2 * items * SB * width * 8,
            transcendentals=0,
        ),
    )(tiles, uvw_columns, lane_rows)


def split(x):
    high = x.astype(jnp.bfloat16)
    return high, (x - high.astype(jnp.float32)).astype(jnp.bfloat16)


def dot(left, right, left_dim, right_dim):
    def one(a, b):
        return lax.dot_general(
            a,
            b,
            (((left_dim,), (right_dim,)), ((), ())),
            preferred_element_type=jnp.float32,
        )

    return one(left[0], right[0]) + (one(left[0], right[1]) + one(left[1], right[0]))


def normal_kernel(
    tiles_ref, grow_ref, gcol_ref, cos_ref, sin_ref, vis_ref, w_ref, flux_ref, out_ref
):
    item = pl.program_id(0)

    @pl.when(item == 0)
    def _():
        out_ref[...] = jnp.zeros_like(out_ref)

    width = flux_ref.shape[1]
    row_block = tiles_ref[item, 0]
    col_block = tiles_ref[item, 1]
    weights = jnp.concatenate([w_ref[0]] * 4, axis=0)
    own = (
        lax.broadcasted_iota(jnp.int32, (LANES, LANES), 0) // SB
        == lax.broadcasted_iota(jnp.int32, (LANES, LANES), 1) // SB
    )
    mask = own.astype(jnp.float32)
    mask_half = mask.astype(jnp.bfloat16)
    for start in range(0, width, LANES):
        re = slice(start, start + LANES)
        im = slice(width + start, width + start + LANES)
        flux = flux_ref[:, re]
        cr, sr = cos_ref[0, :, re], sin_ref[0, :, re]
        cc, sc = cos_ref[1, :, re], sin_ref[1, :, re]
        a_re, a_im = grow_ref[0, :, re], grow_ref[0, :, im]
        b_re, b_im = gcol_ref[0, :, re], gcol_ref[0, :, im]
        row_re, row_im = split(a_re * cr - a_im * sr), split(a_re * sr + a_im * cr)
        col_re = split(flux * (b_re * cc - b_im * sc))
        col_im = split(flux * (b_re * sc + b_im * cc))
        rows = [
            jnp.concatenate(
                [
                    jnp.concatenate([row_re[j]] * 4, axis=0) * mask_half,
                    jnp.concatenate([row_im[j]] * 4, axis=0) * mask_half,
                ],
                axis=1,
            )
            for j in range(2)
        ]
        cols = [
            jnp.concatenate(
                [
                    jnp.concatenate([col_re[j], col_im[j]], axis=1),
                    jnp.concatenate([-col_im[j], col_re[j]], axis=1),
                ],
                axis=0,
            )
            for j in range(2)
        ]
        model = dot(rows, cols, 1, 1)
        observed = vis_ref[0, start : start + LANES, :].astype(jnp.float32)
        resid = split((observed - model) * weights)
        srow = dot(resid, cols, 1, 0)
        cross = dot(resid, rows, 0, 0)
        s_re, s_im = srow[:, :LANES] * mask, srow[:, LANES:] * mask
        s_re = (s_re[0:32] + s_re[32:64]) + (s_re[64:96] + s_re[96:128])
        s_im = (s_im[0:32] + s_im[32:64]) + (s_im[64:96] + s_im[96:128])
        t_re = flux * (cross[:SB, :LANES] + cross[SB:, LANES:])
        t_im = flux * (cross[:SB, LANES:] - cross[SB:, :LANES])
        out_ref[row_block, :, re] += cr * s_re + sr * s_im
        out_ref[row_block, :, im] += cr * s_im - sr * s_re
        out_ref[col_block, :, re] += cc * t_re + sc * t_im
        out_ref[col_block, :, im] += cc * t_im - sc * t_re


def normal_terms(group, tiles, gathered, cosine, sine_part, vis_rows, weights, flux_row):
    items = tiles.shape[0]
    width = flux_row.shape[1]
    blocks = gathered.shape[0]
    gain_spec = lambda side: pl.BlockSpec(
        (1, SB, 2 * width), lambda i, t: (t[i, side], 0, 0)
    )
    turn_spec = pl.BlockSpec((2, SB, width), lambda i, t: (i, 0, group))
    return pl.pallas_call(
        normal_kernel,
        grid_spec=pltpu.PrefetchScalarGridSpec(
            num_scalar_prefetch=1,
            grid=(items,),
            in_specs=[
                gain_spec(0),
                gain_spec(1),
                turn_spec,
                turn_spec,
                pl.BlockSpec((1, width, 2 * SB), lambda i, t: (i, group, 0)),
                pl.BlockSpec((1, SB, 2 * SB), lambda i, t: (i, 0, 0)),
                pl.BlockSpec((1, width), lambda i, t: (0, 0)),
            ],
            out_specs=pl.BlockSpec((blocks, SB, 2 * width), lambda i, t: (0, 0, 0)),
        ),
        out_shape=jax.ShapeDtypeStruct((blocks, SB, 2 * width), jnp.float32),
        compiler_params=pltpu.CompilerParams(vmem_limit_bytes=VMEM),
        cost_estimate=pl.CostEstimate(
            flops=items * width * 3 * 8 * SB * SB * 24,
            bytes_accessed=items * width * SB * 30 + blocks * SB * width * 8,
            transcendentals=0,
        ),
    )(tiles, gathered, gathered, cosine, sine_part, vis_rows, weights, flux_row)


class Line:
    def __init__(self, count):
        chips = count // 2
        self.cols = 1
        while (2 * self.cols) ** 2 <= chips:
            self.cols *= 2
        self.rows = chips // self.cols
        me = lax.axis_index("tile")
        self.me = me
        self.c = lax.rem(me, 2)
        self.b = lax.rem(me // 2, self.cols)
        self.a = me // (2 * self.cols)

    def index(self, a, b, c):
        return (a * self.cols + b) * 2 + c

    def has_row(self, a):
        return (a >= 0) & (a < self.rows)

    def has_col(self, b):
        return (b >= 0) & (b < self.cols)

    def greet(self):
        barrier = pltpu.get_barrier_semaphore()
        near = [(self.a + d, self.b, self.has_row(self.a + d)) for d in (1, -1)]
        near += [(self.a, self.b + d, self.has_col(self.b + d)) for d in (1, -1)]
        total = 1
        pl.semaphore_signal(
            barrier, inc=1, device_id={"tile": self.index(self.a, self.b, 1 - self.c)}
        )
        for a, b, there in near:
            total = total + there.astype(jnp.int32)

            @pl.when(there)
            def _():
                pl.semaphore_signal(
                    barrier, inc=1, device_id={"tile": self.index(a, b, self.c)}
                )

        pl.semaphore_wait(barrier, total)


def signed(distance):
    return [(distance, 1), (distance, -1)] if distance else [(0, 0)]


UP, DOWN, RIGHT, LEFT, CORE = range(5)


def gather_kernel(count, arrays, *refs):
    ins, outs = refs[:arrays], refs[arrays : 2 * arrays]
    send, recv = refs[2 * arrays :]
    at = Line(count)
    for n in range(arrays):
        outs[n][at.me] = ins[n][...]
    at.greet()

    def copies(origin, target, way):
        return [
            pltpu.make_async_remote_copy(
                src_ref=outs[n].at[origin],
                dst_ref=outs[n].at[origin],
                send_sem=send.at[n, way, origin],
                recv_sem=recv.at[n, origin],
                device_id={"tile": target},
            )
            for n in range(arrays)
        ]

    partner = at.index(at.a, at.b, 1 - at.c)

    def visit(finish):
        def emit(origin, target, way):
            for copy in copies(origin, target, way):
                if finish:
                    copy.wait_send()
                else:
                    copy.start()

        for clock in range(at.rows + at.cols - 1):
            for s in range(max(0, clock - at.cols + 1), min(clock, at.rows - 1) + 1):
                for s_, va in signed(s):
                    for t_, vb in signed(clock - s):
                        a, b = at.a - s_ * va, at.b - t_ * vb

                        @pl.when(at.has_row(a) & at.has_col(b))
                        def _():
                            origin = at.index(a, b, at.c)
                            if clock and not finish:
                                for copy in copies(origin, partner, CORE):
                                    copy.wait_recv()
                            if t_ == 0:
                                for way, step in ((UP, 1), (DOWN, -1)):
                                    if va in (0, step):

                                        @pl.when(at.has_row(at.a + step))
                                        def _():
                                            emit(origin, at.index(at.a + step, at.b, at.c), way)

                            for way, step in ((RIGHT, 1), (LEFT, -1)):
                                if vb in (0, step):

                                    @pl.when(at.has_col(at.b + step))
                                    def _():
                                        emit(origin, at.index(at.a, at.b + step, at.c), way)

                            emit(origin, partner, CORE)

    visit(False)
    for chip in range(at.rows * at.cols):
        for copy in copies(2 * chip + 1 - at.c, partner, CORE):
            copy.wait_recv()
    visit(True)


def gather_all(count, call, *arrays):
    number = len(arrays)
    return pl.pallas_call(
        functools.partial(gather_kernel, count, number),
        out_shape=[jax.ShapeDtypeStruct((count,) + x.shape, x.dtype) for x in arrays],
        in_specs=[pl.BlockSpec(memory_space=pltpu.VMEM)] * number,
        out_specs=[pl.BlockSpec(memory_space=pltpu.VMEM)] * number,
        scratch_shapes=[
            pltpu.SemaphoreType.DMA((number, 5, count)),
            pltpu.SemaphoreType.DMA((number, count)),
        ],
        compiler_params=pltpu.CompilerParams(
            collective_id=call, has_side_effects=True, vmem_limit_bytes=VMEM
        ),
    )(*arrays)


def scatter_kernel(
    count, x, out, from_core, from_col, to_col, from_row, to_row,
    core_send, core_recv, col_send, col_recv, row_send, row_recv
):
    at = Line(count)
    at.greet()
    partner = at.index(at.a, at.b, 1 - at.c)

    def core_copy(chip):
        return pltpu.make_async_remote_copy(
            src_ref=x.at[2 * chip + 1 - at.c],
            dst_ref=from_core.at[chip],
            send_sem=core_send.at[chip],
            recv_sem=core_recv.at[chip],
            device_id={"tile": partner},
        )

    def col_copy(chip, way, step):
        return pltpu.make_async_remote_copy(
            src_ref=to_col.at[chip],
            dst_ref=from_col.at[way, chip],
            send_sem=col_send.at[chip],
            recv_sem=col_recv.at[way, chip],
            device_id={"tile": at.index(at.a, at.b + step, at.c)},
        )

    def row_copy(a, way, step):
        return pltpu.make_async_remote_copy(
            src_ref=to_row.at[a],
            dst_ref=from_row.at[way, a],
            send_sem=row_send.at[a],
            recv_sem=row_recv.at[way, a],
            device_id={"tile": at.index(at.a + step, at.b, at.c)},
        )

    def each_row(body):
        for s in reversed(range(at.rows)):
            for s_, va in signed(s):
                a = at.a + s_ * va

                @pl.when(at.has_row(a))
                def _():
                    body(a, va)

    def each_far_col(body):
        for t in reversed(range(1, at.cols)):
            for t_, vb in signed(t):
                b = at.b + t_ * vb

                @pl.when(at.has_col(b))
                def _():
                    body(b, vb)

    def start_core(a, va):
        each_far_col(lambda b, vb: core_copy(a * at.cols + b).start())

    def start_core_near(a, va):
        core_copy(a * at.cols + at.b).start()

    each_row(start_core)
    each_row(start_core_near)

    def pass_col(a, va):
        def far(b, vb):
            chip = a * at.cols + b
            core_copy(chip).wait_recv()
            to_col[chip] = x[2 * chip + at.c] + from_core[chip]
            way = 0 if vb > 0 else 1

            @pl.when(at.has_col(at.b - vb))
            def _():
                col_copy(chip, way, vb).wait_recv()
                to_col[chip] += from_col[way, chip]

            col_copy(chip, way, vb).start()

        each_far_col(far)

    each_row(pass_col)

    def pass_row(a, va):
        chip = a * at.cols + at.b
        core_copy(chip).wait_recv()
        to_row[a] = x[2 * chip + at.c] + from_core[chip]
        for way, step in ((0, 1), (1, -1)):

            @pl.when(at.has_col(at.b - step))
            def _():
                col_copy(chip, way, step).wait_recv()
                to_row[a] += from_col[way, chip]

        for way, step in ((0, 1), (1, -1)):
            if va in (0, step):

                @pl.when(at.has_row(at.a - step))
                def _():
                    row_copy(a, way, step).wait_recv()
                    to_row[a] += from_row[way, a]

        if va == 0:
            out[...] = to_row[a]
        else:
            row_copy(a, 0 if va > 0 else 1, va).start()

    each_row(pass_row)

    def finish(a, va):
        each_far_col(lambda b, vb: col_copy(a * at.cols + b, 0, vb).wait_send())
        if va:
            row_copy(a, 0, va).wait_send()

    each_row(finish)
    for chip in range(at.rows * at.cols):
        core_copy(chip).wait_send()


def scatter_sum(count, call, x):
    piece = x.shape[1:]
    chips = count // 2
    cols = 1
    while (2 * cols) ** 2 <= chips:
        cols *= 2
    rows = chips // cols
    slots = lambda *lead: pltpu.VMEM(lead + piece, x.dtype)
    return pl.pallas_call(
        functools.partial(scatter_kernel, count),
        out_shape=jax.ShapeDtypeStruct(piece, x.dtype),
        in_specs=[pl.BlockSpec(memory_space=pltpu.VMEM)],
        out_specs=pl.BlockSpec(memory_space=pltpu.VMEM),
        scratch_shapes=[
            slots(chips),
            slots(2, chips),
            slots(chips),
            slots(2, rows),
            slots(rows),
            pltpu.SemaphoreType.DMA((chips,)),
            pltpu.SemaphoreType.DMA((chips,)),
            pltpu.SemaphoreType.DMA((chips,)),
            pltpu.SemaphoreType.DMA((2, chips)),
            pltpu.SemaphoreType.DMA((rows,)),
            pltpu.SemaphoreType.DMA((2, rows)),
        ],
        compiler_params=pltpu.CompilerParams(
            collective_id=call, has_side_effects=True, vmem_limit_bytes=VMEM
        ),
    )(x)


def on_device(count, gains, tiles, vis, flags, station_uvw, src_lm, flux):
    dirs, chans = flux.shape
    times, _, stations = station_uvw.shape
    items = tiles.shape[0]
    blocks = stations // SB
    owned_count = gains.shape[0] // dirs
    per = chans // GROUPS
    width = per * dirs

    turned = gains.reshape(owned_count, dirs, 2, GROUPS, per).transpose(3, 0, 2, 4, 1)
    owned = [turned[g].reshape(owned_count, 2 * width) for g in range(GROUPS)]

    keep = jnp.logical_or(
        (tiles[:, 0] != tiles[:, 1])[:, None],
        (jnp.arange(SB)[:, None] > jnp.arange(SB)[None, :]).reshape(1, SB * SB),
    )
    weights = jnp.where(keep, flags, 0).astype(jnp.float32)
    extra = jnp.pad(tiles.astype(jnp.float32), ((0, 0), (0, LANES - 3)))
    full_gains, described = gather_all(
        count, 0, owned[0], jnp.concatenate([weights, extra], axis=1)
    )
    gathered = [full_gains.reshape(stations, 2 * width)]
    described = described.reshape(count * items, SB * SB + LANES)
    all_weights = described[:, : SB * SB]
    all_tiles = described[:, SB * SB : SB * SB + 3].astype(jnp.int32)

    source_l, source_m = src_lm[0], src_lm[1]
    squares = source_l * source_l + source_m * source_m
    source_n = -squares / (1.0 + jnp.sqrt(1.0 - squares))
    frequency = 1.0 + jnp.arange(chans, dtype=jnp.float32) / chans
    lane_rows = jnp.stack(
        [jnp.tile(source_l, chans), jnp.tile(source_m, chans), jnp.tile(source_n, chans)]
        + [jnp.repeat(frequency, dirs)] * 5
    )
    uvw_columns = station_uvw.reshape(times, 3, blocks, SB).transpose(0, 2, 3, 1)
    cosine, sine_part = phasors(tiles, uvw_columns, lane_rows)

    vis_rows = vis.reshape(items, 2, chans, SB, SB).transpose(0, 2, 3, 1, 4)
    vis_rows = vis_rows.reshape(items, chans * SB, 2 * SB)
    square = weights.reshape(items, SB, SB)
    pair_weights = jnp.concatenate([square, square], axis=2)
    flux_rows = flux.T.reshape(GROUPS, 1, width)

    first = lax.axis_index("tile") * owned_count
    block, offset = first // SB, first % SB
    labels = jnp.arange(blocks, dtype=jnp.int32)[None, :]
    is_row = (all_tiles[:, 0:1] == block) & (all_tiles[:, 1:2] == labels)
    is_col = (all_tiles[:, 1:2] == block) & (all_tiles[:, 0:1] == labels)
    as_row = jnp.einsum(
        "ib,ix->bx", is_row.astype(jnp.float32), all_weights, precision=highest
    ).reshape(blocks, SB, SB)
    as_col = jnp.einsum(
        "ib,ix->bx", is_col.astype(jnp.float32), all_weights, precision=highest
    ).reshape(blocks, SB, SB)
    as_row = lax.dynamic_slice_in_dim(as_row, offset, owned_count, 1)
    as_col = lax.dynamic_slice_in_dim(as_col, offset, owned_count, 2)
    pair_counts = (as_row.transpose(1, 0, 2) + as_col.transpose(2, 0, 1)).reshape(
        owned_count, stations
    )

    for iteration in range(ITERS):
        updated = []
        for g in range(GROUPS):
            full = gathered[g]
            numerator = normal_terms(
                g,
                tiles,
                full.reshape(blocks, SB, 2 * width),
                cosine,
                sine_part,
                vis_rows,
                pair_weights,
                flux_rows[g],
            ).reshape(count, owned_count, 2 * width)
            share = scatter_sum(count, 2, numerator)
            power = full[:, :width] * full[:, :width] + full[:, width:] * full[:, width:]
            denominator = (flux_rows[g] * flux_rows[g]) * jnp.dot(
                pair_counts, power, precision=highest
            )
            scale = 0.5 / (denominator + 1.0)
            updated.append(owned[g] + share * jnp.concatenate([scale, scale], axis=1))
        owned = updated
        if iteration + 1 < ITERS:
            (full_gains,) = gather_all(count, 1, owned[0])
            gathered = [full_gains.reshape(stations, 2 * width)]

    stacked = jnp.stack(owned).reshape(GROUPS, owned_count, 2, per, dirs)
    return stacked.transpose(1, 4, 2, 0, 3).reshape(owned_count * dirs, 2 * chans)


def solution(mesh):
    placed = (
        P(("group", "tile"), None),
        P(("group", "tile"), None),
        P(("group", "tile"), None, None, None),
        P(("group", "tile"), None),
        P("group", None, None),
        P(),
        P(),
    )
    return jax.shard_map(
        functools.partial(on_device, mesh.shape["tile"]), mesh=mesh, in_specs=placed, out_specs=P(("group", "tile"), None), check_vma=False
    )
```

```python
import functools
import math

import jax
import jax.numpy as jnp
from jax import lax
from jax.experimental import pallas as pl
from jax.experimental.pallas import tpu as pltpu
from jax.sharding import PartitionSpec as P

SB = 32
ITERS = 2
GROUPS = 1
LANES = 128
VMEM = 40 * 1024 * 1024

highest = lax.Precision.HIGHEST


def series(first, step, terms):
    out = []
    for j in range(terms):
        degree = first + step * j
        out.append((-1.0) ** j * math.pi**degree / math.factorial(degree))
    return out


SIN = series(1, 2, 7)
COS = series(0, 2, 7)


def horner(coefficients, z):
    total = jnp.full_like(z, coefficients[-1])
    for value in reversed(coefficients[:-1]):
        total = total * z + value
    return total


def phasor_kernel(tiles_ref, uvw_ref, lanes_ref, cos_ref, sin_ref):
    uvw = uvw_ref[0, 0]
    u, v, w = uvw[:, 0:1], uvw[:, 1:2], uvw[:, 2:3]
    width = lanes_ref.shape[1]
    for start in range(0, width, 256):
        cut = slice(start, start + 256)
        delay = u * lanes_ref[0:1, cut] + v * lanes_ref[1:2, cut] + w * lanes_ref[2:3, cut]
        turns = delay * lanes_ref[3:4, cut]
        r = turns - jnp.floor(turns + 0.5)
        z = r * r
        s = r * horner(SIN, z)
        c = horner(COS, z)
        cos_ref[0, :, cut] = 1.0 - 2.0 * s * s
        sin_ref[0, :, cut] = 2.0 * s * c


def phasors(tiles, uvw_columns, lane_rows):
    items = tiles.shape[0]
    width = lane_rows.shape[1]

    def pick(i, t):
        return (t[i // 2, 2], t[i // 2, i % 2], 0, 0)

    shape = jax.ShapeDtypeStruct((2 * items, SB, width), jnp.float32)
    block = pl.BlockSpec((1, SB, width), lambda i, t: (i, 0, 0))
    return pl.pallas_call(
        phasor_kernel,
        grid_spec=pltpu.PrefetchScalarGridSpec(
            num_scalar_prefetch=1,
            grid=(2 * items,),
            in_specs=[
                pl.BlockSpec((1, 1, SB, 3), pick),
                pl.BlockSpec((8, width), lambda i, t: (0, 0)),
            ],
            out_specs=[block, block],
        ),
        out_shape=[shape, shape],
        compiler_params=pltpu.CompilerParams(vmem_limit_bytes=VMEM),
        cost_estimate=pl.CostEstimate(
            flops=2 * items * SB * width * 40,
            bytes_accessed=2 * items * SB * width * 8,
            transcendentals=0,
        ),
    )(tiles, uvw_columns, lane_rows)


def split(x):
    high = x.astype(jnp.bfloat16)
    return high, (x - high.astype(jnp.float32)).astype(jnp.bfloat16)


def dot(left, right, left_dim, right_dim):
    def one(a, b):
        return lax.dot_general(
            a,
            b,
            (((left_dim,), (right_dim,)), ((), ())),
            preferred_element_type=jnp.float32,
        )

    return one(left[0], right[0]) + (one(left[0], right[1]) + one(left[1], right[0]))


def normal_kernel(
    tiles_ref, grow_ref, gcol_ref, cos_ref, sin_ref, vis_ref, w_ref, flux_ref, out_ref
):
    item = pl.program_id(0)

    @pl.when(item == 0)
    def _():
        out_ref[...] = jnp.zeros_like(out_ref)

    width = flux_ref.shape[1]
    row_block = tiles_ref[item, 0]
    col_block = tiles_ref[item, 1]
    weights = jnp.concatenate([w_ref[0]] * 4, axis=0)
    own = (
        lax.broadcasted_iota(jnp.int32, (LANES, LANES), 0) // SB
        == lax.broadcasted_iota(jnp.int32, (LANES, LANES), 1) // SB
    )
    mask = own.astype(jnp.float32)
    mask_half = mask.astype(jnp.bfloat16)
    for start in range(0, width, LANES):
        re = slice(start, start + LANES)
        im = slice(width + start, width + start + LANES)
        flux = flux_ref[:, re]
        cr, sr = cos_ref[0, :, re], sin_ref[0, :, re]
        cc, sc = cos_ref[1, :, re], sin_ref[1, :, re]
        a_re, a_im = grow_ref[0, :, re], grow_ref[0, :, im]
        b_re, b_im = gcol_ref[0, :, re], gcol_ref[0, :, im]
        row_re, row_im = split(a_re * cr - a_im * sr), split(a_re * sr + a_im * cr)
        col_re = split(flux * (b_re * cc - b_im * sc))
        col_im = split(flux * (b_re * sc + b_im * cc))
        rows = [
            jnp.concatenate(
                [
                    jnp.concatenate([row_re[j]] * 4, axis=0) * mask_half,
                    jnp.concatenate([row_im[j]] * 4, axis=0) * mask_half,
                ],
                axis=1,
            )
            for j in range(2)
        ]
        cols = [
            jnp.concatenate(
                [
                    jnp.concatenate([col_re[j], col_im[j]], axis=1),
                    jnp.concatenate([-col_im[j], col_re[j]], axis=1),
                ],
                axis=0,
            )
            for j in range(2)
        ]
        model = dot(rows, cols, 1, 1)
        seen = slice(start, start + LANES)
        observed = jnp.concatenate(
            [vis_ref[0, 0, seen, :].astype(jnp.float32), vis_ref[0, 1, seen, :].astype(jnp.float32)],
            axis=1,
        )
        resid = split((observed - model) * weights)
        srow = dot(resid, cols, 1, 0)
        cross = dot(resid, rows, 0, 0)
        s_re, s_im = srow[:, :LANES] * mask, srow[:, LANES:] * mask
        s_re = (s_re[0:32] + s_re[32:64]) + (s_re[64:96] + s_re[96:128])
        s_im = (s_im[0:32] + s_im[32:64]) + (s_im[64:96] + s_im[96:128])
        t_re = flux * (cross[:SB, :LANES] + cross[SB:, LANES:])
        t_im = flux * (cross[:SB, LANES:] - cross[SB:, :LANES])
        out_ref[row_block, :, re] += cr * s_re + sr * s_im
        out_ref[row_block, :, im] += cr * s_im - sr * s_re
        out_ref[col_block, :, re] += cc * t_re + sc * t_im
        out_ref[col_block, :, im] += cc * t_im - sc * t_re


def normal_terms(group, tiles, gathered, cosine, sine_part, vis_rows, weights, flux_row):
    items = tiles.shape[0]
    width = flux_row.shape[1]
    blocks = gathered.shape[0]
    gain_spec = lambda side: pl.BlockSpec(
        (1, SB, 2 * width), lambda i, t: (t[i, side], 0, 0)
    )
    turn_spec = pl.BlockSpec((2, SB, width), lambda i, t: (i, 0, group))
    return pl.pallas_call(
        normal_kernel,
        grid_spec=pltpu.PrefetchScalarGridSpec(
            num_scalar_prefetch=1,
            grid=(items,),
            in_specs=[
                gain_spec(0),
                gain_spec(1),
                turn_spec,
                turn_spec,
                pl.BlockSpec((1, 2, width, SB), lambda i, t: (i, 0, group, 0)),
                pl.BlockSpec((1, SB, 2 * SB), lambda i, t: (i, 0, 0)),
                pl.BlockSpec((1, width), lambda i, t: (0, 0)),
            ],
            out_specs=pl.BlockSpec((blocks, SB, 2 * width), lambda i, t: (0, 0, 0)),
        ),
        out_shape=jax.ShapeDtypeStruct((blocks, SB, 2 * width), jnp.float32),
        compiler_params=pltpu.CompilerParams(vmem_limit_bytes=VMEM),
        cost_estimate=pl.CostEstimate(
            flops=items * width * 3 * 8 * SB * SB * 24,
            bytes_accessed=items * width * SB * 30 + blocks * SB * width * 8,
            transcendentals=0,
        ),
    )(tiles, gathered, gathered, cosine, sine_part, vis_rows, weights, flux_row)


class Line:
    def __init__(self, count):
        chips = count // 2
        self.cols = 1
        while (2 * self.cols) ** 2 <= chips:
            self.cols *= 2
        self.rows = chips // self.cols
        me = lax.axis_index("tile")
        self.me = me
        self.c = lax.rem(me, 2)
        self.b = lax.rem(me // 2, self.cols)
        self.a = me // (2 * self.cols)

    def index(self, a, b, c):
        return (a * self.cols + b) * 2 + c

    def has_row(self, a):
        return (a >= 0) & (a < self.rows)

    def has_col(self, b):
        return (b >= 0) & (b < self.cols)

    def greet(self):
        barrier = pltpu.get_barrier_semaphore()
        near = [(self.a + d, self.b, self.has_row(self.a + d)) for d in (1, -1)]
        near += [(self.a, self.b + d, self.has_col(self.b + d)) for d in (1, -1)]
        total = 1
        pl.semaphore_signal(
            barrier, inc=1, device_id={"tile": self.index(self.a, self.b, 1 - self.c)}
        )
        for a, b, there in near:
            total = total + there.astype(jnp.int32)

            @pl.when(there)
            def _():
                pl.semaphore_signal(
                    barrier, inc=1, device_id={"tile": self.index(a, b, self.c)}
                )

        pl.semaphore_wait(barrier, total)


def signed(distance):
    return [(distance, 1), (distance, -1)] if distance else [(0, 0)]


UP, DOWN, RIGHT, LEFT, CORE = range(5)


def gather_kernel(count, arrays, *refs):
    ins, outs = refs[:arrays], refs[arrays : 2 * arrays]
    send, recv = refs[2 * arrays :]
    at = Line(count)
    for n in range(arrays):
        outs[n][at.me] = ins[n][...]
    at.greet()

    def copies(origin, target, way):
        return [
            pltpu.make_async_remote_copy(
                src_ref=outs[n].at[origin],
                dst_ref=outs[n].at[origin],
                send_sem=send.at[n, way, origin],
                recv_sem=recv.at[n, origin],
                device_id={"tile": target},
            )
            for n in range(arrays)
        ]

    partner = at.index(at.a, at.b, 1 - at.c)

    def visit(finish):
        def emit(origin, target, way):
            for copy in copies(origin, target, way):
                if finish:
                    copy.wait_send()
                else:
                    copy.start()

        for clock in range(at.rows + at.cols - 1):
            for s in range(max(0, clock - at.cols + 1), min(clock, at.rows - 1) + 1):
                for s_, va in signed(s):
                    for t_, vb in signed(clock - s):
                        a, b = at.a - s_ * va, at.b - t_ * vb

                        @pl.when(at.has_row(a) & at.has_col(b))
                        def _():
                            origin = at.index(a, b, at.c)
                            if clock and not finish:
                                for copy in copies(origin, partner, CORE):
                                    copy.wait_recv()
                            if t_ == 0:
                                for way, step in ((UP, 1), (DOWN, -1)):
                                    if va in (0, step):

                                        @pl.when(at.has_row(at.a + step))
                                        def _():
                                            emit(origin, at.index(at.a + step, at.b, at.c), way)

                            for way, step in ((RIGHT, 1), (LEFT, -1)):
                                if vb in (0, step):

                                    @pl.when(at.has_col(at.b + step))
                                    def _():
                                        emit(origin, at.index(at.a, at.b + step, at.c), way)

                            emit(origin, partner, CORE)

    visit(False)
    for chip in range(at.rows * at.cols):
        for copy in copies(2 * chip + 1 - at.c, partner, CORE):
            copy.wait_recv()
    visit(True)


def gather_all(count, call, *arrays):
    number = len(arrays)
    return pl.pallas_call(
        functools.partial(gather_kernel, count, number),
        out_shape=[jax.ShapeDtypeStruct((count,) + x.shape, x.dtype) for x in arrays],
        in_specs=[pl.BlockSpec(memory_space=pltpu.VMEM)] * number,
        out_specs=[pl.BlockSpec(memory_space=pltpu.VMEM)] * number,
        scratch_shapes=[
            pltpu.SemaphoreType.DMA((number, 5, count)),
            pltpu.SemaphoreType.DMA((number, count)),
        ],
        compiler_params=pltpu.CompilerParams(
            collective_id=call, has_side_effects=True, vmem_limit_bytes=VMEM
        ),
    )(*arrays)


def scatter_kernel(
    count, x, out, from_core, from_col, to_col, from_row, to_row,
    core_send, core_recv, col_send, col_recv, row_send, row_recv
):
    at = Line(count)
    at.greet()
    partner = at.index(at.a, at.b, 1 - at.c)

    def core_copy(chip):
        return pltpu.make_async_remote_copy(
            src_ref=x.at[2 * chip + 1 - at.c],
            dst_ref=from_core.at[chip],
            send_sem=core_send.at[chip],
            recv_sem=core_recv.at[chip],
            device_id={"tile": partner},
        )

    def col_copy(chip, way, step):
        return pltpu.make_async_remote_copy(
            src_ref=to_col.at[chip],
            dst_ref=from_col.at[way, chip],
            send_sem=col_send.at[chip],
            recv_sem=col_recv.at[way, chip],
            device_id={"tile": at.index(at.a, at.b + step, at.c)},
        )

    def row_copy(a, way, step):
        return pltpu.make_async_remote_copy(
            src_ref=to_row.at[a],
            dst_ref=from_row.at[way, a],
            send_sem=row_send.at[a],
            recv_sem=row_recv.at[way, a],
            device_id={"tile": at.index(at.a + step, at.b, at.c)},
        )

    def each_row(body):
        for s in reversed(range(at.rows)):
            for s_, va in signed(s):
                a = at.a + s_ * va

                @pl.when(at.has_row(a))
                def _():
                    body(a, va)

    def each_far_col(body):
        for t in reversed(range(1, at.cols)):
            for t_, vb in signed(t):
                b = at.b + t_ * vb

                @pl.when(at.has_col(b))
                def _():
                    body(b, vb)

    def start_core(a, va):
        each_far_col(lambda b, vb: core_copy(a * at.cols + b).start())

    def start_core_near(a, va):
        core_copy(a * at.cols + at.b).start()

    each_row(start_core)
    each_row(start_core_near)

    def pass_col(a, va):
        def far(b, vb):
            chip = a * at.cols + b
            core_copy(chip).wait_recv()
            to_col[chip] = x[2 * chip + at.c] + from_core[chip]
            way = 0 if vb > 0 else 1

            @pl.when(at.has_col(at.b - vb))
            def _():
                col_copy(chip, way, vb).wait_recv()
                to_col[chip] += from_col[way, chip]

            col_copy(chip, way, vb).start()

        each_far_col(far)

    each_row(pass_col)

    def pass_row(a, va):
        chip = a * at.cols + at.b
        core_copy(chip).wait_recv()
        to_row[a] = x[2 * chip + at.c] + from_core[chip]
        for way, step in ((0, 1), (1, -1)):

            @pl.when(at.has_col(at.b - step))
            def _():
                col_copy(chip, way, step).wait_recv()
                to_row[a] += from_col[way, chip]

        for way, step in ((0, 1), (1, -1)):
            if va in (0, step):

                @pl.when(at.has_row(at.a - step))
                def _():
                    row_copy(a, way, step).wait_recv()
                    to_row[a] += from_row[way, a]

        if va == 0:
            out[...] = to_row[a]
        else:
            row_copy(a, 0 if va > 0 else 1, va).start()

    each_row(pass_row)

    def finish(a, va):
        each_far_col(lambda b, vb: col_copy(a * at.cols + b, 0, vb).wait_send())
        if va:
            row_copy(a, 0, va).wait_send()

    each_row(finish)
    for chip in range(at.rows * at.cols):
        core_copy(chip).wait_send()


def scatter_sum(count, call, x):
    piece = x.shape[1:]
    chips = count // 2
    cols = 1
    while (2 * cols) ** 2 <= chips:
        cols *= 2
    rows = chips // cols
    slots = lambda *lead: pltpu.VMEM(lead + piece, x.dtype)
    return pl.pallas_call(
        functools.partial(scatter_kernel, count),
        out_shape=jax.ShapeDtypeStruct(piece, x.dtype),
        in_specs=[pl.BlockSpec(memory_space=pltpu.VMEM)],
        out_specs=pl.BlockSpec(memory_space=pltpu.VMEM),
        scratch_shapes=[
            slots(chips),
            slots(2, chips),
            slots(chips),
            slots(2, rows),
            slots(rows),
            pltpu.SemaphoreType.DMA((chips,)),
            pltpu.SemaphoreType.DMA((chips,)),
            pltpu.SemaphoreType.DMA((chips,)),
            pltpu.SemaphoreType.DMA((2, chips)),
            pltpu.SemaphoreType.DMA((rows,)),
            pltpu.SemaphoreType.DMA((2, rows)),
        ],
        compiler_params=pltpu.CompilerParams(
            collective_id=call, has_side_effects=True, vmem_limit_bytes=VMEM
        ),
    )(x)


def on_device(count, gains, tiles, vis, flags, station_uvw, src_lm, flux):
    dirs, chans = flux.shape
    times, _, stations = station_uvw.shape
    items = tiles.shape[0]
    blocks = stations // SB
    owned_count = gains.shape[0] // dirs
    per = chans // GROUPS
    width = per * dirs

    turned = gains.reshape(owned_count, dirs, 2, GROUPS, per).transpose(3, 0, 2, 4, 1)
    owned = [turned[g].reshape(owned_count, 2 * width) for g in range(GROUPS)]

    keep = jnp.logical_or(
        (tiles[:, 0] != tiles[:, 1])[:, None],
        (jnp.arange(SB)[:, None] > jnp.arange(SB)[None, :]).reshape(1, SB * SB),
    )
    weights = jnp.where(keep, flags, 0).astype(jnp.float32)
    extra = jnp.pad(tiles.astype(jnp.float32), ((0, 0), (0, LANES - 3)))
    full_gains, described = gather_all(
        count, 0, owned[0], jnp.concatenate([weights, extra], axis=1)
    )
    gathered = [full_gains.reshape(stations, 2 * width)]
    described = described.reshape(count * items, SB * SB + LANES)
    all_weights = described[:, : SB * SB]
    all_tiles = described[:, SB * SB : SB * SB + 3].astype(jnp.int32)

    source_l, source_m = src_lm[0], src_lm[1]
    squares = source_l * source_l + source_m * source_m
    source_n = -squares / (1.0 + jnp.sqrt(1.0 - squares))
    frequency = 1.0 + jnp.arange(chans, dtype=jnp.float32) / chans
    lane_rows = jnp.stack(
        [jnp.tile(source_l, chans), jnp.tile(source_m, chans), jnp.tile(source_n, chans)]
        + [jnp.repeat(frequency, dirs)] * 5
    )
    uvw_columns = station_uvw.reshape(times, 3, blocks, SB).transpose(0, 2, 3, 1)
    cosine, sine_part = phasors(tiles, uvw_columns, lane_rows)

    vis_rows = vis.reshape(items, 2, chans * SB, SB)
    square = weights.reshape(items, SB, SB)
    pair_weights = jnp.concatenate([square, square], axis=2)
    flux_rows = flux.T.reshape(GROUPS, 1, width)

    first = lax.axis_index("tile") * owned_count
    block, offset = first // SB, first % SB
    labels = jnp.arange(blocks, dtype=jnp.int32)[None, :]
    is_row = (all_tiles[:, 0:1] == block) & (all_tiles[:, 1:2] == labels)
    is_col = (all_tiles[:, 1:2] == block) & (all_tiles[:, 0:1] == labels)
    as_row = jnp.einsum(
        "ib,ix->bx", is_row.astype(jnp.float32), all_weights, precision=highest
    ).reshape(blocks, SB, SB)
    as_col = jnp.einsum(
        "ib,ix->bx", is_col.astype(jnp.float32), all_weights, precision=highest
    ).reshape(blocks, SB, SB)
    as_row = lax.dynamic_slice_in_dim(as_row, offset, owned_count, 1)
    as_col = lax.dynamic_slice_in_dim(as_col, offset, owned_count, 2)
    pair_counts = (as_row.transpose(1, 0, 2) + as_col.transpose(2, 0, 1)).reshape(
        owned_count, stations
    )

    for iteration in range(ITERS):
        updated = []
        for g in range(GROUPS):
            full = gathered[g]
            numerator = normal_terms(
                g,
                tiles,
                full.reshape(blocks, SB, 2 * width),
                cosine,
                sine_part,
                vis_rows,
                pair_weights,
                flux_rows[g],
            ).reshape(count, owned_count, 2 * width)
            share = scatter_sum(count, 2, numerator)
            power = full[:, :width] * full[:, :width] + full[:, width:] * full[:, width:]
            denominator = (flux_rows[g] * flux_rows[g]) * jnp.dot(
                pair_counts, power, precision=highest
            )
            scale = 0.5 / (denominator + 1.0)
            updated.append(owned[g] + share * jnp.concatenate([scale, scale], axis=1))
        owned = updated
        if iteration + 1 < ITERS:
            (full_gains,) = gather_all(count, 1, owned[0])
            gathered = [full_gains.reshape(stations, 2 * width)]

    stacked = jnp.stack(owned).reshape(GROUPS, owned_count, 2, per, dirs)
    return stacked.transpose(1, 4, 2, 0, 3).reshape(owned_count * dirs, 2 * chans)


def solution(mesh):
    placed = (
        P(("group", "tile"), None),
        P(("group", "tile"), None),
        P(("group", "tile"), None, None, None),
        P(("group", "tile"), None),
        P("group", None, None),
        P(),
        P(),
    )
    return jax.shard_map(
        functools.partial(on_device, mesh.shape["tile"]), mesh=mesh, in_specs=placed, out_specs=P(("group", "tile"), None), check_vma=False
    )
```
